512 devices in a mesh: dp: 128 (over x_hi, z, y), fsdp: 4 (over x_lo, core).
Axes of the slice: x: 4 (x_hi: 2, x_lo: 2; x = x_hi * 2 + x_lo), y: 4, z: 16, core: 2. Of those that a mesh axis runs over, the one named last changes fastest.
Arguments:
- caption_encoder_outputs: bfloat16 [24576, 1152], P(('dp', 'fsdp')), may hold values from -6 to 6
- picture_vectors: bfloat16 [24576, 1152], P(('dp', 'fsdp')), may hold values from -6 to 6
- caption_mapping_weights: bfloat16 [1152, 1152], P('fsdp'), may hold values from -0.1875 to 0.1875
- natural_exponent_coldness: float32 [1], replicated, may hold values from 4.3 to 4.7
- offset_constant: float32 [1], replicated, may hold values from -8 to -5
- objective_weighting: float32 [1], replicated, may hold values from 4096 to 16384
Outputs:
- feat_grad: bfloat16 [24576, 1152], P(('dp', 'fsdp'))
- head_grad: float32 [128, 1152, 1152], P('dp', 'fsdp')
The draws below stay inside these ranges and needn't reach their ends.
All inputs are finite; a program needn't handle non-finite values.
Results may differ from the reference program's by a relative error of at most 0.035.
Values may be sent and summed in bfloat16 or wider, within the bound.
No kernel may reach another device: no remote copies, remote signals or barrier semaphores. Data moves between devices by JAX's collectives and lax.ppermute only.
A program may use at most 64 MiB of HBM per device.

```python
import math
import jax
import jax.numpy as jnp
from jax import lax

D = 1152
ROWS = 48
BATCH = 24576
N_DP = 128
N_FSDP = 4


def block_levels(key, dims, shards, least, top_value):
    def one(position, shards_of):
        heights = jax.random.uniform(jax.random.fold_in(jax.random.fold_in(key, 6), position), (shards_of,), jnp.float32, least / len(shards), top_value / len(shards))
        return jnp.repeat(jnp.exp(heights), dims[position] // shards_of).reshape((-1,) + (1,) * (len(dims) - position - 1))

    factor_of = one(*shards[0])
    for cut in shards[1:]:
        factor_of = factor_of * one(*cut)
    return factor_of


def bell_draw(stream_key, shape, deviation, most, cuts=(), held_as=jnp.bfloat16):
    values = deviation * jax.random.normal(stream_key, shape, jnp.float32)
    if cuts:
        values = values * block_levels(stream_key, shape, cuts, -0.22, 0.18)
    return jnp.clip(values, -most, most).astype(held_as)


def setup_inputs(seed: int = 0) -> dict:
    splits = jax.random.split(jax.random.key(seed), 7)
    caption_encoder_outputs = bell_draw(splits[0], (BATCH, D), 1.0, 6.0, ((0, 512),))
    picture_vectors = bell_draw(splits[1], (BATCH, D), 1.0, 6.0, ((0, 512),))
    caption_mapping_weights = bell_draw(splits[2], (D, D), D ** -0.5, 0.1875, ((0, 4),))
    natural_exponent_coldness = jnp.clip(jax.random.uniform(splits[3], (1,), jnp.float32, 4.3, 4.7), 4.3, 4.7)
    offset_constant = jnp.clip(jax.random.uniform(splits[4], (1,), jnp.float32, -8.0, -5.0), -8.0, -5.0)
    objective_weighting = jnp.clip(jnp.exp(jax.random.uniform(splits[5], (1,), jnp.float32, math.log(4096.0), math.log(16384.0))), 4096.0, 16384.0)
    return {"caption_encoder_outputs": caption_encoder_outputs, "picture_vectors": picture_vectors, "caption_mapping_weights": caption_mapping_weights, "natural_exponent_coldness": natural_exponent_coldness, "offset_constant": offset_constant, "objective_weighting": objective_weighting}


epsilon = 1e-06

def reference(caption_encoder_outputs, picture_vectors, caption_mapping_weights, natural_exponent_coldness, offset_constant, objective_weighting):
    example_total_number = caption_encoder_outputs.shape[0]
    group_rows = N_FSDP * ROWS
    projected = jnp.dot(caption_encoder_outputs, caption_mapping_weights, preferred_element_type=jnp.float32)
    text_norm = jnp.sqrt(lax.optimization_barrier(jnp.sum(projected * projected, axis=-1, keepdims=True)) + epsilon)
    unit_text = projected / text_norm
    text_embed = unit_text.astype(jnp.bfloat16)
    image_vals = picture_vectors.astype(jnp.float32)
    image_norm = jnp.sqrt(lax.optimization_barrier(jnp.sum(image_vals * image_vals, axis=-1, keepdims=True)) + epsilon)
    image_embed = (image_vals / image_norm).astype(jnp.bfloat16)
    sharpness_factor = jnp.exp(natural_exponent_coldness[0])
    added_offset_entry = offset_constant[0]
    derivative_factor = sharpness_factor * objective_weighting[0] / example_total_number
    image_ids = jnp.arange(example_total_number, dtype=jnp.int32)

    def score_block(inputs):
        block_text, first_row = inputs
        cosine_agreement = jnp.dot(block_text, image_embed.T, preferred_element_type=jnp.float32)
        cross_affinity_table = sharpness_factor * cosine_agreement + added_offset_entry
        text_ids = first_row + jnp.arange(group_rows, dtype=jnp.int32)
        labels = jnp.where(text_ids[:, None] == image_ids[None, :], 1.0, -1.0).astype(jnp.float32)
        weights = (-labels * jax.nn.sigmoid(-labels * cross_affinity_table) * derivative_factor).astype(jnp.bfloat16)
        return jnp.dot(weights, image_embed, preferred_element_type=jnp.float32)
    firsts = jnp.arange(N_DP, dtype=jnp.int32) * group_rows
    embed_grad = lax.map(score_block, (text_embed.reshape(N_DP, group_rows, D), firsts)).reshape(example_total_number, D)
    radial = lax.optimization_barrier(jnp.sum(unit_text * embed_grad, axis=-1, keepdims=True))
    proj_grad = ((embed_grad - unit_text * radial) / text_norm).astype(jnp.bfloat16)
    feat_grad = jnp.dot(proj_grad, caption_mapping_weights.T, preferred_element_type=jnp.float32).astype(jnp.bfloat16)

    def group_grad(inputs):
        group_feats, group_grads = inputs
        partials = jnp.einsum('frk,frl->fkl', group_feats.astype(jnp.float32), group_grads.astype(jnp.float32))
        rounded = lax.optimization_barrier(partials.astype(jnp.bfloat16))
        return lax.optimization_barrier(jnp.sum(rounded.astype(jnp.float32), axis=0))
    head_grad = lax.map(group_grad, (caption_encoder_outputs.reshape(N_DP, N_FSDP, ROWS, D), proj_grad.reshape(N_DP, N_FSDP, ROWS, D)))
    return (feat_grad, head_grad)
```

```python
import jax
import jax.numpy as jnp
from jax import lax
from jax.sharding import Mesh, PartitionSpec as P

AXES = ("xh", "z", "y", "xl", "c")
SIZES = (2, 16, 4, 2, 2)
PLANE = ("xh", "y", "xl")
LINE = ("z", "c")
RING = ("xh", "xl")
FSDP = ("xl", "c")

epsilon = 1e-06


def shift(step, size):
    return [(i, (i + step) % size) for i in range(size)]


def whole_head(rows):
    half = rows.shape[0] // 2
    other = jnp.concatenate(
        [
            lax.ppermute(rows[:half], RING, shift(1, 4)),
            lax.ppermute(rows[half:], RING, shift(3, 4)),
        ]
    )
    mine = jnp.stack([rows, other])
    theirs = lax.ppermute(mine, "c", shift(1, 2))
    chip, core = lax.axis_index("xl"), lax.axis_index("c")
    low = jnp.where(core == 0, mine, theirs)
    high = jnp.where(core == 0, theirs, mine)
    first = jnp.concatenate([low[0], high[0]])
    second = jnp.concatenate([low[1], high[1]])
    return jnp.where(
        chip == 0, jnp.concatenate([first, second]), jnp.concatenate([second, first])
    )


def body(features, pictures, head_rows, coldness, offset, weighting):
    rows, width = features.shape
    xh, z, y, xl, c = (lax.axis_index(a) for a in AXES)
    total_rows = rows * 512

    image_vals = pictures.astype(jnp.float32)
    image_norm = jnp.sqrt(jnp.sum(image_vals * image_vals, axis=-1, keepdims=True) + epsilon)
    image_embed = (image_vals / image_norm).astype(jnp.bfloat16)
    images = lax.all_gather(image_embed, LINE, axis=0, tiled=True)

    head = whole_head(head_rows)
    columns = lax.all_to_all(features, FSDP, 1, 0, tiled=True)
    plane_features = lax.all_to_all(jnp.tile(features, (16, 1)), PLANE, 0, 0, tiled=True)

    projected = jnp.dot(plane_features, head, preferred_element_type=jnp.float32)
    plane_norm = jnp.sqrt(jnp.sum(projected * projected, axis=-1, keepdims=True) + epsilon)
    plane_unit = projected / plane_norm
    plane_text = plane_unit.astype(jnp.bfloat16)
    place = ((xh * 4 + y) * 2 + xl) * rows
    unit_text = lax.dynamic_slice_in_dim(plane_unit, place, rows)
    text_norm = lax.dynamic_slice_in_dim(plane_norm, place, rows)

    sharpness = jnp.exp(coldness[0])
    factor = sharpness * weighting[0] / total_rows

    r = jnp.arange(rows, dtype=jnp.int32)
    plane_at = jnp.arange(16, dtype=jnp.int32)
    text_at = (((plane_at // 8) * 16 + z) * 4 + plane_at // 2 % 4) * 4 + plane_at % 2 * 2 + c
    line_at = jnp.arange(32, dtype=jnp.int32)
    image_at = ((xh * 16 + line_at // 2) * 4 + y) * 4 + xl * 2 + line_at % 2
    text_ids = (text_at[:, None] * rows + r[None, :]).reshape(-1)
    image_ids = (image_at[:, None] * rows + r[None, :]).reshape(-1)

    cosine = lax.dot_general(
        plane_text, images, (((1,), (1,)), ((), ())), preferred_element_type=jnp.float32
    )
    logits = sharpness * cosine + offset[0]
    labels = jnp.where(text_ids[:, None] == image_ids[None, :], 1.0, -1.0).astype(jnp.float32)
    weights = (-labels * jax.nn.sigmoid(-labels * logits) * factor).astype(jnp.bfloat16)
    partial = jnp.dot(weights, images, preferred_element_type=jnp.float32).astype(jnp.bfloat16)

    parts = lax.all_to_all(partial, PLANE, 0, 0, tiled=True).reshape(16, rows, width)
    own_grad = jnp.sum(parts.astype(jnp.float32), axis=0)
    radial = jnp.sum(unit_text * own_grad, axis=-1, keepdims=True)
    proj_grad = ((own_grad - unit_text * radial) / text_norm).astype(jnp.bfloat16)
    feat_grad = lax.dot_general(
        proj_grad, head, (((1,), (1,)), ((), ())), preferred_element_type=jnp.float32
    )
    group_grad = lax.all_gather(proj_grad, FSDP, axis=0, tiled=True)
    head_grad = lax.dot_general(
        columns, group_grad, (((0,), (0,)), ((), ())), preferred_element_type=jnp.float32
    )
    return feat_grad.astype(jnp.bfloat16), head_grad[None]


def solution(mesh):
    fine = Mesh(mesh.devices.reshape(SIZES), AXES)
    return jax.shard_map(
        body,
        mesh=fine,
        in_specs=(P(AXES, None), P(AXES, None), P(FSDP, None), P(), P(), P()),
        out_specs=(P(AXES, None), P(("xh", "z", "y"), FSDP, None)),
        check_vma=False,
    )
```

```python
import functools

import jax
import jax.numpy as jnp
from jax import lax
from jax.experimental import pallas as pl
from jax.experimental.pallas import tpu as pltpu
from jax.sharding import Mesh, PartitionSpec as P

AXES = ("xh", "za", "zb", "y", "xl", "c")
SIZES = (2, 4, 4, 4, 2, 2)
LINE = ("za", "zb")
PLANE = ("xh", "y", "xl")
RING = ("xh", "xl")
FSDP = ("xl", "c")

epsilon = 1e-06
LOG2E = 1.4426950408889634
WIDE = 256
VMEM_BYTES = 18 * 2**20
BY_COLUMNS = (((1,), (1,)), ((), ()))

IN_VMEM = pl.BlockSpec(memory_space=pltpu.VMEM)
IN_SMEM = pl.BlockSpec(memory_space=pltpu.SMEM)
ANYWHERE = pl.BlockSpec(memory_space=pl.ANY)


def shift(step, size):
    return [(i, (i + step) % size) for i in range(size)]


def along_z(array, step):
    return lax.ppermute(array, LINE, shift(step % 16, 16))


def other_core(array):
    return lax.ppermute(array, "c", shift(1, 2))


def lay(pieces, whole_ref, sems, starts):
    copies = [
        pltpu.make_async_copy(piece, whole_ref.at[pl.ds(start, piece.shape[0])], sems.at[k])
        for k, (piece, start) in enumerate(zip(pieces, starts))
    ]
    for copy in copies:
        copy.start()
    for copy in copies:
        copy.wait()


def unit_kernel(rows_ref, out_ref):
    values = rows_ref[...].astype(jnp.float32)
    norm = jnp.sqrt(jnp.sum(values * values, axis=-1, keepdims=True) + epsilon)
    out_ref[...] = (values / norm).astype(out_ref.dtype)


def unit_rows(rows):
    return pl.pallas_call(
        unit_kernel,
        out_shape=jax.ShapeDtypeStruct(rows.shape, rows.dtype),
        in_specs=[IN_VMEM],
        out_specs=IN_VMEM,
        compiler_params=pltpu.CompilerParams(vmem_limit_bytes=2**21),
    )(rows)


def project_kernel(block, place_ref, from_ref, *refs):
    pieces, (text_ref, head_ref, pair_ref, rows_ref, sems, rows_sem) = refs[:-6], refs[-6:]
    copy = pltpu.make_async_copy(from_ref, rows_ref, rows_sem)
    copy.start()
    depth = pieces[0].shape[0]
    starts = [pl.multiple_of(place_ref[k] * depth, 32) for k in range(len(pieces))]
    lay(pieces, head_ref, sems, starts)
    copy.wait()
    for start in range(0, rows_ref.shape[0], block):
        at = pl.ds(start, block)
        projected = jnp.dot(rows_ref[at], head_ref[...], preferred_element_type=jnp.float32)
        norm = jnp.sqrt(jnp.sum(projected * projected, axis=-1, keepdims=True) + epsilon)
        text_ref[at] = (projected * (1.0 / norm)).astype(text_ref.dtype)
    count = pair_ref.shape[0]
    pair_ref[...] = rows_ref[pl.ds(pl.multiple_of(place_ref[len(pieces)] * count, 32), count)]


def project(place, rows, pieces, pair):
    count, width = rows.shape
    return pl.pallas_call(
        functools.partial(project_kernel, count // 2),
        out_shape=[
            jax.ShapeDtypeStruct((count, width), jnp.bfloat16),
            jax.ShapeDtypeStruct((width, width), jnp.bfloat16),
            jax.ShapeDtypeStruct((pair, width), jnp.bfloat16),
        ],
        in_specs=[IN_SMEM] + [ANYWHERE] * (1 + len(pieces)),
        out_specs=[IN_VMEM] * 3,
        scratch_shapes=[
            pltpu.VMEM((count, width), jnp.bfloat16),
            pltpu.SemaphoreType.DMA((len(pieces),)),
            pltpu.SemaphoreType.DMA,
        ],
        compiler_params=pltpu.CompilerParams(vmem_limit_bytes=VMEM_BYTES),
        cost_estimate=pl.CostEstimate(
            flops=2 * count * width * width,
            bytes_accessed=4 * width * (count + width),
            transcendentals=0,
        ),
    )(place, rows, *pieces)


def meet_kernel(block, own_rows, added, scalars_ref, place_ref, text_ref, *refs):
    pieces, (out_ref, images_ref, sems) = refs[:-3], refs[-3:]
    if added:
        pieces, sum_ref = pieces[:-1], pieces[-1]
    starts = [sum(p.shape[0] for p in pieces[:k]) for k in range(len(pieces))]
    lay(pieces, images_ref, sems, starts)
    scale, plus, minus, rest = (scalars_ref[k] for k in range(4))
    for start in range(0, text_ref.shape[0], block):
        at = pl.ds(start, block)
        cosine = lax.dot_general(
            text_ref[at], images_ref[...], BY_COLUMNS, preferred_element_type=jnp.float32
        )
        weights = 1.0 / (jnp.exp2(plus - cosine * scale) + rest)
        if own_rows:
            text = lax.broadcasted_iota(jnp.int32, (block, WIDE), 0) + (start - place_ref[0])
            image = lax.broadcasted_iota(jnp.int32, (block, WIDE), 1) - place_ref[1]
            paired = -1.0 / (jnp.exp2(cosine[:, :WIDE] * scale + minus) + rest)
            own = (text == image) & (text >= 0) & (text < own_rows)
            first = jnp.where(own, paired, weights[:, :WIDE])
            weights = jnp.concatenate([first, weights[:, WIDE:]], axis=1)
        grad = jnp.dot(
            weights.astype(jnp.bfloat16), images_ref[...], preferred_element_type=jnp.float32
        )
        if added:
            grad = sum_ref[at] + grad
        out_ref[at] = grad.astype(out_ref.dtype)


def meet(scalars, place, text, pieces, total=None, own_rows=0, dtype=jnp.float32):
    count, width = text.shape
    images = sum(p.shape[0] for p in pieces)
    given = () if total is None else (total,)
    return pl.pallas_call(
        functools.partial(meet_kernel, count // 2, own_rows, len(given)),
        out_shape=jax.ShapeDtypeStruct((count, width), dtype),
        in_specs=[IN_SMEM, IN_SMEM, IN_VMEM]
        + [ANYWHERE] * len(pieces)
        + [IN_VMEM] * len(given),
        out_specs=IN_VMEM,
        scratch_shapes=[
            pltpu.VMEM((images, width), jnp.bfloat16),
            pltpu.SemaphoreType.DMA((len(pieces),)),
        ],
        compiler_params=pltpu.CompilerParams(vmem_limit_bytes=VMEM_BYTES),
        cost_estimate=pl.CostEstimate(
            flops=4 * count * images * width,
            bytes_accessed=2 * width * (3 * count + images),
            transcendentals=2 * count * images,
        ),
    )(scalars, place, text, *pieces, *given)


def join_kernel(*refs):
    pieces, (out_ref, sems) = refs[:-3], refs[-2:]
    lay(pieces, out_ref, sems, [sum(p.shape[0] for p in pieces[:k]) for k in range(len(pieces))])


def join(pieces, after):
    count, width = sum(p.shape[0] for p in pieces), pieces[0].shape[1]
    return pl.pallas_call(
        join_kernel,
        out_shape=jax.ShapeDtypeStruct((count, width), jnp.bfloat16),
        in_specs=[ANYWHERE] * (len(pieces) + 1),
        out_specs=ANYWHERE,
        scratch_shapes=[pltpu.SemaphoreType.DMA((len(pieces),))],
        compiler_params=pltpu.CompilerParams(vmem_limit_bytes=2**20),
        cost_estimate=pl.CostEstimate(
            flops=0, bytes_accessed=4 * count * width, transcendentals=0
        ),
    )(*pieces, after)


def finish_kernel(parts_ref, projected_ref, out_ref):
    projected = projected_ref[...]
    norm = jnp.sqrt(jnp.sum(projected * projected, axis=-1, keepdims=True) + epsilon)
    unit = projected / norm
    grad = parts_ref[0].astype(jnp.float32)
    for k in range(1, parts_ref.shape[0]):
        grad = grad + parts_ref[k].astype(jnp.float32)
    radial = jnp.sum(unit * grad, axis=-1, keepdims=True)
    out_ref[...] = ((grad - unit * radial) / norm).astype(out_ref.dtype)


def finish(parts, projected):
    return pl.pallas_call(
        finish_kernel,
        out_shape=jax.ShapeDtypeStruct(projected.shape, jnp.bfloat16),
        in_specs=[IN_VMEM, IN_VMEM],
        out_specs=IN_VMEM,
        compiler_params=pltpu.CompilerParams(vmem_limit_bytes=VMEM_BYTES // 2),
    )(parts, projected)


def body(features, pictures, head_rows, coldness, offset, weighting):
    rows, width = features.shape
    xh, za, zb, y, xl, c = (lax.axis_index(a) for a in AXES)
    plane = 16
    place = (((xh * 4 + y) * 2 + xl) * rows).astype(jnp.int32)

    plane_features = lax.all_to_all(jnp.tile(features, (plane, 1)), PLANE, 0, 0, tiled=True)

    crossed = lax.ppermute(head_rows, "xl", shift(1, 2))
    head_pieces = [head_rows, crossed, other_core(head_rows), other_core(crossed)]
    at = [(xl * 2 + c), ((1 - xl) * 2 + c), (xl * 2 + 1 - c), ((1 - xl) * 2 + 1 - c), xh * 4 + y]
    head_place = jnp.stack([a.astype(jnp.int32) for a in at])

    own = unit_rows(pictures)
    quarter = lax.all_gather(own, "za", axis=0, tiled=True)
    half = quarter.shape[0] // 2
    late = [
        along_z(quarter, 1),
        along_z(quarter, -1),
        along_z(quarter[:half], 2),
        along_z(quarter[half:], -2),
    ]
    early = [quarter, other_core(quarter)]

    text, head, pair = project(head_place, plane_features, head_pieces, 2 * rows)

    sharpness = jnp.exp(coldness[0])
    factor = sharpness * weighting[0] / (rows * 512)
    log_factor = jnp.log2(factor)
    shift_up = offset[0] * LOG2E
    scalars = jnp.stack(
        [sharpness * LOG2E, -shift_up - log_factor, shift_up - log_factor, 1.0 / factor]
    )
    places = jnp.stack([place, (za * rows).astype(jnp.int32)])
    total = meet(scalars, places, text, early, own_rows=rows)
    late = join(late, total)
    late_other = other_core(late)
    total = meet(scalars, places, text, [late], total)
    partial = meet(scalars, places, text, [late_other], total, dtype=jnp.bfloat16)

    parts = lax.all_to_all(partial, PLANE, 0, 0, tiled=True).reshape(plane, rows, width)

    projected = jnp.dot(features, head, preferred_element_type=jnp.float32)
    other = other_core(pair)
    low, high = jnp.where(c == 0, pair, other), jnp.where(c == 0, other, pair)
    group = jnp.stack([low.reshape(2, rows, width), high.reshape(2, rows, width)], axis=1)
    columns = lax.dynamic_slice_in_dim(
        group.reshape(4 * rows, width), (xl * 2 + c) * (width // 4), width // 4, axis=1
    )

    proj_grad = finish(parts, projected)
    feat_grad = lax.dot_general(proj_grad, head, BY_COLUMNS, preferred_element_type=jnp.float32)
    group_grad = lax.all_gather(proj_grad, FSDP, axis=0, tiled=True)
    head_grad = lax.dot_general(
        columns, group_grad, (((0,), (0,)), ((), ())), preferred_element_type=jnp.float32
    )
    return feat_grad.astype(jnp.bfloat16), head_grad[None]


def solution(mesh):
    fine = Mesh(mesh.devices.reshape(SIZES), AXES)
    return jax.shard_map(
        body,
        mesh=fine,
        in_specs=(P(AXES, None), P(AXES, None), P(FSDP, None), P(), P(), P()),
        out_specs=(P(AXES, None), P(("xh", "za", "zb", "y"), FSDP, None)),
        check_vma=False,
    )
```

```python
import functools

import jax
import jax.numpy as jnp
from jax import lax
from jax.experimental import pallas as pl
from jax.experimental.pallas import tpu as pltpu
from jax.sharding import Mesh, PartitionSpec as P

AXES = ("xh", "za", "zb", "y", "xl", "c")
SIZES = (2, 4, 4, 4, 2, 2)
LINE = ("za", "zb")
PLANE = ("xh", "y", "xl")
RING = ("xh", "xl")
FSDP = ("xl", "c")

epsilon = 1e-06
LOG2E = 1.4426950408889634
TOTAL_ROWS = 24576
VMEM_BYTES = 18 * 2**20
BY_COLUMNS = (((1,), (1,)), ((), ()))

IN_VMEM = pl.BlockSpec(memory_space=pltpu.VMEM)
IN_SMEM = pl.BlockSpec(memory_space=pltpu.SMEM)
ANYWHERE = pl.BlockSpec(memory_space=pl.ANY)
IN_HBM = pl.BlockSpec(memory_space=pltpu.HBM)


def shift(step, size):
    return [(i, (i + step) % size) for i in range(size)]


def along_z(array, step):
    return lax.ppermute(array, LINE, shift(step % 16, 16))


def other_core(array):
    return lax.ppermute(array, "c", shift(1, 2))


def lay(pieces, whole_ref, sems, starts):
    copies = [
        pltpu.make_async_copy(piece, whole_ref.at[pl.ds(start, piece.shape[0])], sems.at[k])
        for k, (piece, start) in enumerate(zip(pieces, starts))
    ]
    for copy in copies:
        copy.start()
    for copy in copies:
        copy.wait()


def unit_kernel(rows_ref, out_ref):
    values = rows_ref[...].astype(jnp.float32)
    norm = jnp.sqrt(jnp.sum(values * values, axis=-1, keepdims=True) + epsilon)
    out_ref[...] = (values / norm).astype(out_ref.dtype)


def unit_rows(rows):
    return pl.pallas_call(
        unit_kernel,
        out_shape=jax.ShapeDtypeStruct(rows.shape, rows.dtype),
        in_specs=[IN_VMEM],
        out_specs=IN_VMEM,
        compiler_params=pltpu.CompilerParams(vmem_limit_bytes=2**21),
    )(rows)


def project_kernel(block, place_ref, from_ref, *refs):
    settings, pieces, refs = refs[:3], refs[3:-7], refs[-7:]
    text_ref, head_ref, pair_ref, scalars_ref, rows_ref, sems, rows_sem = refs
    copy = pltpu.make_async_copy(from_ref, rows_ref, rows_sem)
    copy.start()
    depth = pieces[0].shape[0]
    starts = [pl.multiple_of(place_ref[k] * depth, 32) for k in range(len(pieces))]
    lay(pieces, head_ref, sems, starts)
    copy.wait()
    for start in range(0, rows_ref.shape[0], block):
        at = pl.ds(start, block)
        projected = jnp.dot(rows_ref[at], head_ref[...], preferred_element_type=jnp.float32)
        norm = jnp.sqrt(jnp.sum(projected * projected, axis=-1, keepdims=True) + epsilon)
        text_ref[at] = (projected * (1.0 / norm)).astype(text_ref.dtype)
    coldness, offset, weighting = (setting[...] for setting in settings)
    sharpness = jnp.exp(coldness)
    factor = sharpness * weighting * (1.0 / TOTAL_ROWS)
    raised, log_factor = offset * LOG2E, jnp.log2(factor)
    scalars = [sharpness * LOG2E, -raised - log_factor, raised - log_factor, 1.0 / factor]
    for k, scalar in enumerate(scalars):
        scalars_ref[k : k + 1] = jnp.broadcast_to(scalar, (1, scalars_ref.shape[1]))
    count = pair_ref.shape[0]
    pair_ref[...] = rows_ref[pl.ds(pl.multiple_of(place_ref[len(pieces)] * count, 32), count)]


def project(place, rows, settings, pieces, pair):
    count, width = rows.shape
    return pl.pallas_call(
        functools.partial(project_kernel, count // 2),
        out_shape=[
            jax.ShapeDtypeStruct((count, width), jnp.bfloat16),
            jax.ShapeDtypeStruct((width, width), jnp.bfloat16),
            jax.ShapeDtypeStruct((pair, width), jnp.bfloat16),
            jax.ShapeDtypeStruct((8, 128), jnp.float32),
        ],
        in_specs=[IN_SMEM, IN_HBM] + [IN_VMEM] * 3 + [ANYWHERE] * len(pieces),
        out_specs=[IN_VMEM] * 4,
        scratch_shapes=[
            pltpu.VMEM((count, width), jnp.bfloat16),
            pltpu.SemaphoreType.DMA((len(pieces),)),
            pltpu.SemaphoreType.DMA,
        ],
        compiler_params=pltpu.CompilerParams(vmem_limit_bytes=46 * 2**20),
    )(place, rows, *settings, *pieces)


def meet_kernel(block, own_rows, last, place_ref, text_ref, *refs):
    scalars_ref, refs = refs[0], refs[1:]
    if last:
        pieces, (sum_ref, _, into_ref, images_ref, sems, out_ref, out_sems) = refs[:-7], refs[-7:]
    else:
        pieces, (out_ref, images_ref, sems) = refs[:-3], refs[-3:]
        if not own_rows:
            pieces, sum_ref = pieces[:-1], pieces[-1]
    lay(pieces, images_ref, sems, [sum(p.shape[0] for p in pieces[:k]) for k in range(len(pieces))])
    scale, plus, minus, rest = (scalars_ref[k : k + 1, :1] for k in range(4))

    def result(k):
        at = pl.ds(pl.multiple_of(k * block, block), block)
        return pltpu.make_async_copy(out_ref.at[at], into_ref.at[at], out_sems.at[k])

    def step(k, _):
        at = pl.ds(pl.multiple_of(k * block, block), block)
        cosine = lax.dot_general(
            text_ref[at], images_ref[...], BY_COLUMNS, preferred_element_type=jnp.float32
        )
        weights = 1.0 / (jnp.exp2(plus - cosine * scale) + rest)
        grad = jnp.dot(
            weights.astype(jnp.bfloat16), images_ref[...], preferred_element_type=jnp.float32
        )
        if not own_rows:
            grad = sum_ref[at] + grad
        out_ref[at] = grad.astype(out_ref.dtype)
        if last:
            result(k).start()
        return 0

    steps = text_ref.shape[0] // block
    lax.fori_loop(0, steps, step, 0)
    if own_rows:
        own = pl.ds(pl.multiple_of(place_ref[5], 16), own_rows)
        image = images_ref[pl.ds(pl.multiple_of(place_ref[6], 16), own_rows)].astype(jnp.float32)
        cosine = jnp.sum(text_ref[own].astype(jnp.float32) * image, axis=-1, keepdims=True)
        apart = 1.0 / (jnp.exp2(plus - cosine * scale) + rest)
        paired = -1.0 / (jnp.exp2(cosine * scale + minus) + rest)
        change = paired.astype(jnp.bfloat16).astype(jnp.float32)
        change = change - apart.astype(jnp.bfloat16).astype(jnp.float32)
        out_ref[own] = out_ref[own] + change * image
    if last:
        for k in range(steps):
            result(k).wait()


def meet(scalars, place, text, pieces, total=None, into=None, own_rows=0):
    count, width = text.shape
    images = sum(p.shape[0] for p in pieces)
    last = into is not None
    given = [a for a in (total, into) if a is not None]
    return pl.pallas_call(
        functools.partial(meet_kernel, count // 2, own_rows, last),
        out_shape=jax.ShapeDtypeStruct((count, width), jnp.bfloat16 if last else jnp.float32),
        in_specs=[IN_SMEM, IN_VMEM]
        + [IN_VMEM]
        + [ANYWHERE] * len(pieces)
        + [IN_VMEM, IN_HBM][: len(given)],
        out_specs=IN_HBM if last else IN_VMEM,
        scratch_shapes=[
            pltpu.VMEM((images, width), jnp.bfloat16),
            pltpu.SemaphoreType.DMA((len(pieces),)),
        ]
        + ([pltpu.VMEM((count, width), jnp.bfloat16), pltpu.SemaphoreType.DMA((2,))] if last else []),
        input_output_aliases={4 + len(pieces): 0} if last else {},
        compiler_params=pltpu.CompilerParams(vmem_limit_bytes=VMEM_BYTES),
        cost_estimate=pl.CostEstimate(
            flops=4 * count * images * width,
            bytes_accessed=2 * width * (3 * count + images),
            transcendentals=2 * count * images,
        ),
    )(place, text, scalars, *pieces, *given)


def join_kernel(*refs):
    pieces, (out_ref, sems) = refs[:-3], refs[-2:]
    lay(pieces, out_ref, sems, [sum(p.shape[0] for p in pieces[:k]) for k in range(len(pieces))])


def join(pieces, after):
    count, width = sum(p.shape[0] for p in pieces), pieces[0].shape[1]
    return pl.pallas_call(
        join_kernel,
        out_shape=jax.ShapeDtypeStruct((count, width), jnp.bfloat16),
        in_specs=[ANYWHERE] * (len(pieces) + 1),
        out_specs=ANYWHERE,
        scratch_shapes=[pltpu.SemaphoreType.DMA((len(pieces),))],
        compiler_params=pltpu.CompilerParams(vmem_limit_bytes=2**20),
        cost_estimate=pl.CostEstimate(
            flops=0, bytes_accessed=4 * count * width, transcendentals=0
        ),
    )(*pieces, after)


def finish_kernel(parts_ref, projected_ref, out_ref):
    projected = projected_ref[...]
    norm = jnp.sqrt(jnp.sum(projected * projected, axis=-1, keepdims=True) + epsilon)
    unit = projected / norm
    grad = parts_ref[0].astype(jnp.float32)
    for k in range(1, parts_ref.shape[0]):
        grad = grad + parts_ref[k].astype(jnp.float32)
    radial = jnp.sum(unit * grad, axis=-1, keepdims=True)
    out_ref[...] = ((grad - unit * radial) / norm).astype(out_ref.dtype)


def finish(parts, projected):
    return pl.pallas_call(
        finish_kernel,
        out_shape=jax.ShapeDtypeStruct(projected.shape, jnp.bfloat16),
        in_specs=[IN_VMEM, IN_VMEM],
        out_specs=IN_VMEM,
        compiler_params=pltpu.CompilerParams(vmem_limit_bytes=VMEM_BYTES // 2),
    )(parts, projected)


def body(features, pictures, head_rows, coldness, offset, weighting):
    rows, width = features.shape
    xh, za, zb, y, xl, c = (lax.axis_index(a) for a in AXES)
    plane = 16
    place = (((xh * 4 + y) * 2 + xl) * rows).astype(jnp.int32)

    plane_features = lax.all_to_all(jnp.tile(features, (plane, 1)), PLANE, 0, 0, tiled=True)

    crossed = lax.ppermute(head_rows, "xl", shift(1, 2))
    at = [xl * 2 + c, (1 - xl) * 2 + c, xl * 2 + 1 - c, (1 - xl) * 2 + 1 - c]
    at += [xh * 4 + y, place, za * rows]
    places = jnp.stack([a.astype(jnp.int32) for a in at])

    own = unit_rows(pictures)
    quarter = lax.all_gather(own, "za", axis=0, tiled=True)
    half = quarter.shape[0] // 2
    late = [
        along_z(quarter, 1),
        along_z(quarter, -1),
        along_z(quarter[:half], 2),
        along_z(quarter[half:], -2),
    ]
    head_pieces = [head_rows, crossed, other_core(head_rows), other_core(crossed)]
    settings = [setting.reshape(1, 1) for setting in (coldness, offset, weighting)]
    text, head, pair, scalars = project(places, plane_features, settings, head_pieces, 2 * rows)

    line = join([quarter] + late, text)
    other_line = other_core(line)
    total = meet(scalars, places, text, [line], own_rows=rows)
    partial = meet(scalars, places, text, [other_line], total, plane_features)

    parts = lax.all_to_all(partial, PLANE, 0, 0, tiled=True).reshape(plane, rows, width)

    projected = jnp.dot(features, head, preferred_element_type=jnp.float32)
    other = other_core(pair)
    low, high = jnp.where(c == 0, pair, other), jnp.where(c == 0, other, pair)
    group = jnp.stack([low.reshape(2, rows, width), high.reshape(2, rows, width)], axis=1)
    columns = lax.dynamic_slice_in_dim(
        group.reshape(4 * rows, width), (xl * 2 + c) * (width // 4), width // 4, axis=1
    )

    proj_grad = finish(parts, projected)
    group_grad = lax.all_gather(proj_grad, FSDP, axis=0, tiled=True)
    proj_grad, _ = lax.optimization_barrier((proj_grad, group_grad))
    feat_grad = lax.dot_general(proj_grad, head, BY_COLUMNS, preferred_element_type=jnp.float32)
    head_grad = lax.dot_general(
        columns, group_grad, (((0,), (0,)), ((), ())), preferred_element_type=jnp.float32
    )
    return feat_grad.astype(jnp.bfloat16), head_grad[None]


def solution(mesh):
    fine = Mesh(mesh.devices.reshape(SIZES), AXES)
    return jax.shard_map(
        body,
        mesh=fine,
        in_specs=(P(AXES, None), P(AXES, None), P(FSDP, None), P(), P(), P()),
        out_specs=(P(AXES, None), P(("xh", "za", "zb", "y"), FSDP, None)),
        check_vma=False,
    )
```

```python
import functools

import jax
import jax.numpy as jnp
from jax import lax
from jax.experimental import pallas as pl
from jax.experimental.pallas import tpu as pltpu
from jax.sharding import Mesh, PartitionSpec as P

AXES = ("xh", "zh", "zl", "y", "xl", "c")
SIZES = (2, 8, 2, 4, 2, 2)
LINE = ("zh", "zl")
PLANE = ("xh", "y", "xl")
RING = ("xh", "xl")
FSDP = ("xl", "c")

epsilon = 1e-06
LOG2E = 1.4426950408889634
TOTAL_ROWS = 24576
VMEM_BYTES = 18 * 2**20
BY_COLUMNS = (((1,), (1,)), ((), ()))
BY_ROWS = (((0,), (0,)), ((), ()))

IN_VMEM = pl.BlockSpec(memory_space=pltpu.VMEM)
IN_SMEM = pl.BlockSpec(memory_space=pltpu.SMEM)
ANYWHERE = pl.BlockSpec(memory_space=pl.ANY)
IN_HBM = pl.BlockSpec(memory_space=pltpu.HBM)


def shift(step, size):
    return [(i, (i + step) % size) for i in range(size)]


def along_z(array, step):
    return lax.ppermute(array, LINE, shift(step % 16, 16))


def other_core(array):
    return lax.ppermute(array, "c", shift(1, 2))


def lay(pieces, whole_ref, sems, starts):
    copies = [
        pltpu.make_async_copy(piece, whole_ref.at[pl.ds(start, piece.shape[0])], sems.at[k])
        for k, (piece, start) in enumerate(zip(pieces, starts))
    ]
    for copy in copies:
        copy.start()
    for copy in copies:
        copy.wait()


def unit_kernel(rows_ref, out_ref):
    values = rows_ref[...].astype(jnp.float32)
    norm = jnp.sqrt(jnp.sum(values * values, axis=-1, keepdims=True) + epsilon)
    out_ref[...] = (values / norm).astype(out_ref.dtype)


def unit_rows(rows):
    return pl.pallas_call(
        unit_kernel,
        out_shape=jax.ShapeDtypeStruct(rows.shape, rows.dtype),
        in_specs=[IN_VMEM],
        out_specs=IN_VMEM,
        compiler_params=pltpu.CompilerParams(vmem_limit_bytes=2**21),
    )(rows)


def project_kernel(block, place_ref, from_ref, *refs):
    settings, pieces, refs = refs[:3], refs[3:-7], refs[-7:]
    text_ref, head_ref, pair_ref, scalars_ref, rows_ref, sems, rows_sem = refs
    copy = pltpu.make_async_copy(from_ref, rows_ref, rows_sem)
    copy.start()
    depth = pieces[0].shape[0]
    starts = [pl.multiple_of(place_ref[k] * depth, 32) for k in range(len(pieces))]
    lay(pieces, head_ref, sems, starts)
    copy.wait()
    for start in range(0, rows_ref.shape[0], block):
        at = pl.ds(start, block)
        projected = jnp.dot(rows_ref[at], head_ref[...], preferred_element_type=jnp.float32)
        norm = jnp.sqrt(jnp.sum(projected * projected, axis=-1, keepdims=True) + epsilon)
        text_ref[at] = (projected * (1.0 / norm)).astype(text_ref.dtype)
    coldness, offset, weighting = (setting[...] for setting in settings)
    sharpness = jnp.exp(coldness)
    factor = sharpness * weighting * (1.0 / TOTAL_ROWS)
    raised, log_factor = offset * LOG2E, jnp.log2(factor)
    scalars = [sharpness * LOG2E, -raised - log_factor, raised - log_factor, 1.0 / factor]
    for k, scalar in enumerate(scalars):
        scalars_ref[k : k + 1] = jnp.broadcast_to(scalar, (1, scalars_ref.shape[1]))
    count = pair_ref.shape[0]
    pair_ref[...] = rows_ref[pl.ds(pl.multiple_of(place_ref[len(pieces)] * count, 32), count)]


def project(place, rows, settings, pieces, pair):
    count, width = rows.shape
    return pl.pallas_call(
        functools.partial(project_kernel, count // 2),
        out_shape=[
            jax.ShapeDtypeStruct((count, width), jnp.bfloat16),
            jax.ShapeDtypeStruct((width, width), jnp.bfloat16),
            jax.ShapeDtypeStruct((pair, width), jnp.bfloat16),
            jax.ShapeDtypeStruct((8, 128), jnp.float32),
        ],
        in_specs=[IN_SMEM, IN_HBM] + [IN_VMEM] * 3 + [ANYWHERE] * len(pieces),
        out_specs=[IN_VMEM] * 4,
        scratch_shapes=[
            pltpu.VMEM((count, width), jnp.bfloat16),
            pltpu.SemaphoreType.DMA((len(pieces),)),
            pltpu.SemaphoreType.DMA,
        ],
        compiler_params=pltpu.CompilerParams(vmem_limit_bytes=46 * 2**20),
    )(place, rows, *settings, *pieces)


def meet_kernel(block, own_rows, last, place_ref, text_ref, *refs):
    scalars_ref, refs = refs[0], refs[1:]
    if last:
        pieces, (sum_ref, _, into_ref, images_ref, sems, out_ref, out_sems) = refs[:-7], refs[-7:]
    else:
        pieces, (out_ref, images_ref, sems) = refs[:-3], refs[-3:]
        if not own_rows:
            pieces, sum_ref = pieces[:-1], pieces[-1]
    lay(pieces, images_ref, sems, [sum(p.shape[0] for p in pieces[:k]) for k in range(len(pieces))])
    scale, plus, minus, rest = (scalars_ref[k : k + 1, :1] for k in range(4))

    def result(k):
        at = pl.ds(pl.multiple_of(k * block, block), block)
        return pltpu.make_async_copy(out_ref.at[at], into_ref.at[at], out_sems.at[k])

    def step(k, _):
        at = pl.ds(pl.multiple_of(k * block, block), block)
        cosine = lax.dot_general(
            text_ref[at], images_ref[...], BY_COLUMNS, preferred_element_type=jnp.float32
        )
        weights = 1.0 / (jnp.exp2(plus - cosine * scale) + rest)
        grad = jnp.dot(
            weights.astype(jnp.bfloat16), images_ref[...], preferred_element_type=jnp.float32
        )
        if not own_rows:
            grad = sum_ref[at] + grad
        out_ref[at] = grad.astype(out_ref.dtype)
        if last:
            result(k).start()
        return 0

    steps = text_ref.shape[0] // block
    lax.fori_loop(0, steps, step, 0)
    if own_rows:
        own = pl.ds(pl.multiple_of(place_ref[5], 16), own_rows)
        image = images_ref[pl.ds(pl.multiple_of(place_ref[6], 16), own_rows)].astype(jnp.float32)
        cosine = jnp.sum(text_ref[own].astype(jnp.float32) * image, axis=-1, keepdims=True)
        apart = 1.0 / (jnp.exp2(plus - cosine * scale) + rest)
        paired = -1.0 / (jnp.exp2(cosine * scale + minus) + rest)
        change = paired.astype(jnp.bfloat16).astype(jnp.float32)
        change = change - apart.astype(jnp.bfloat16).astype(jnp.float32)
        out_ref[own] = out_ref[own] + change * image
    if last:
        for k in range(steps):
            result(k).wait()


def meet(scalars, place, text, pieces, total=None, into=None, own_rows=0):
    count, width = text.shape
    images = sum(p.shape[0] for p in pieces)
    last = into is not None
    given = [a for a in (total, into) if a is not None]
    return pl.pallas_call(
        functools.partial(meet_kernel, count // 2, own_rows, last),
        out_shape=jax.ShapeDtypeStruct((count, width), jnp.bfloat16 if last else jnp.float32),
        in_specs=[IN_SMEM, IN_VMEM]
        + [IN_VMEM]
        + [ANYWHERE] * len(pieces)
        + [IN_VMEM, IN_HBM][: len(given)],
        out_specs=IN_HBM if last else IN_VMEM,
        scratch_shapes=[
            pltpu.VMEM((images, width), jnp.bfloat16),
            pltpu.SemaphoreType.DMA((len(pieces),)),
        ]
        + ([pltpu.VMEM((count, width), jnp.bfloat16), pltpu.SemaphoreType.DMA((2,))] if last else []),
        input_output_aliases={4 + len(pieces): 0} if last else {},
        compiler_params=pltpu.CompilerParams(vmem_limit_bytes=VMEM_BYTES),
        cost_estimate=pl.CostEstimate(
            flops=4 * count * images * width,
            bytes_accessed=2 * width * (3 * count + images),
            transcendentals=2 * count * images,
        ),
    )(place, text, scalars, *pieces, *given)


def join_kernel(*refs):
    pieces, (out_ref, sems) = refs[:-3], refs[-2:]
    lay(pieces, out_ref, sems, [sum(p.shape[0] for p in pieces[:k]) for k in range(len(pieces))])


def join(pieces, after):
    count, width = sum(p.shape[0] for p in pieces), pieces[0].shape[1]
    return pl.pallas_call(
        join_kernel,
        out_shape=jax.ShapeDtypeStruct((count, width), jnp.bfloat16),
        in_specs=[ANYWHERE] * (len(pieces) + 1),
        out_specs=ANYWHERE,
        scratch_shapes=[pltpu.SemaphoreType.DMA((len(pieces),))],
        compiler_params=pltpu.CompilerParams(vmem_limit_bytes=2**20),
        cost_estimate=pl.CostEstimate(
            flops=0, bytes_accessed=4 * count * width, transcendentals=0
        ),
    )(*pieces, after)


def finish_kernel(from_ref, projected_ref, out_ref, parts_ref, sems):
    copies = [
        pltpu.make_async_copy(from_ref.at[k], parts_ref.at[k], sems.at[k])
        for k in range(parts_ref.shape[0])
    ]
    for copy in copies:
        copy.start()
    projected = projected_ref[...]
    norm = jnp.sqrt(jnp.sum(projected * projected, axis=-1, keepdims=True) + epsilon)
    unit = projected / norm
    grad = jnp.zeros(unit.shape, jnp.float32)
    for k, copy in enumerate(copies):
        copy.wait()
        grad = grad + parts_ref[k].astype(jnp.float32)
    radial = jnp.sum(unit * grad, axis=-1, keepdims=True)
    out_ref[...] = ((grad - unit * radial) / norm).astype(out_ref.dtype)


def finish(parts, projected):
    return pl.pallas_call(
        finish_kernel,
        out_shape=jax.ShapeDtypeStruct(projected.shape, jnp.bfloat16),
        in_specs=[ANYWHERE, IN_VMEM],
        out_specs=IN_VMEM,
        scratch_shapes=[
            pltpu.VMEM(parts.shape, parts.dtype),
            pltpu.SemaphoreType.DMA((parts.shape[0],)),
        ],
        compiler_params=pltpu.CompilerParams(vmem_limit_bytes=VMEM_BYTES // 2),
    )(parts, projected)


def last_kernel(columns_ref, group_ref, own_ref, from_ref, feat_ref, to_ref, head_ref, grad_ref, sem, to_sem):
    head = pltpu.make_async_copy(from_ref, head_ref, sem)
    head.start()
    grad_ref[...] = lax.dot_general(
        columns_ref[...], group_ref[...], BY_ROWS, preferred_element_type=jnp.float32
    )
    result = pltpu.make_async_copy(grad_ref, to_ref, to_sem)
    result.start()
    head.wait()
    feat_ref[...] = lax.dot_general(
        own_ref[...], head_ref[...], BY_COLUMNS, preferred_element_type=jnp.float32
    ).astype(feat_ref.dtype)
    result.wait()


def last(columns, group_grad, own_grad, head):
    width = head.shape[0]
    return pl.pallas_call(
        last_kernel,
        out_shape=[
            jax.ShapeDtypeStruct(own_grad.shape, jnp.bfloat16),
            jax.ShapeDtypeStruct((columns.shape[1], width), jnp.float32),
        ],
        in_specs=[IN_VMEM] * 3 + [ANYWHERE],
        out_specs=[IN_VMEM, ANYWHERE],
        scratch_shapes=[
            pltpu.VMEM(head.shape, jnp.bfloat16),
            pltpu.VMEM((columns.shape[1], width), jnp.float32),
            pltpu.SemaphoreType.DMA,
            pltpu.SemaphoreType.DMA,
        ],
        compiler_params=pltpu.CompilerParams(vmem_limit_bytes=VMEM_BYTES),
    )(columns, group_grad, own_grad, head)


def body(features, pictures, head_rows, coldness, offset, weighting):
    rows, width = features.shape
    xh, zh, zl, y, xl, c = (lax.axis_index(a) for a in AXES)
    plane = 16
    place = (((xh * 4 + y) * 2 + xl) * rows).astype(jnp.int32)

    plane_features = lax.all_to_all(jnp.tile(features, (plane, 1)), PLANE, 0, 0, tiled=True)

    crossed = lax.ppermute(head_rows, "xl", shift(1, 2))
    at = [xl * 2 + c, (1 - xl) * 2 + c, xl * 2 + 1 - c, (1 - xl) * 2 + 1 - c]
    at += [xh * 4 + y, place, zh * rows]
    places = jnp.stack([a.astype(jnp.int32) for a in at])

    own = unit_rows(pictures)
    even = lax.all_gather(own, "zh", axis=0, tiled=True)
    half = even.shape[0] // 2
    late = [along_z(even[:half], 1), along_z(even[half:], -1)]
    head_pieces = [head_rows, crossed, other_core(head_rows), other_core(crossed)]
    settings = [setting.reshape(1, 1) for setting in (coldness, offset, weighting)]
    text, head, pair, scalars = project(places, plane_features, settings, head_pieces, 2 * rows)

    line = join([even] + late, text)
    other_line = other_core(line)
    total = meet(scalars, places, text, [line], own_rows=rows)
    partial = meet(scalars, places, text, [other_line], total, plane_features)

    parts = lax.all_to_all(partial, PLANE, 0, 0, tiled=True).reshape(plane, rows, width)

    projected = jnp.dot(features, head, preferred_element_type=jnp.float32)
    other = other_core(pair)
    low, high = jnp.where(c == 0, pair, other), jnp.where(c == 0, other, pair)
    group = jnp.stack([low.reshape(2, rows, width), high.reshape(2, rows, width)], axis=1)
    columns = lax.dynamic_slice_in_dim(
        group.reshape(4 * rows, width), (xl * 2 + c) * (width // 4), width // 4, axis=1
    )

    proj_grad = finish(parts, projected)
    group_grad = lax.all_gather(proj_grad, FSDP, axis=0, tiled=True)
    feat_grad, head_grad = last(columns, group_grad, proj_grad, head)
    return feat_grad, head_grad[None]


def solution(mesh):
    fine = Mesh(mesh.devices.reshape(SIZES), AXES)
    return jax.shard_map(
        body,
        mesh=fine,
        in_specs=(P(AXES, None), P(AXES, None), P(FSDP, None), P(), P(), P()),
        out_specs=(P(AXES, None), P(("xh", "zh", "zl", "y"), FSDP, None)),
        check_vma=False,
    )
```

```python
import functools

import jax
import jax.numpy as jnp
from jax import lax
from jax.experimental import pallas as pl
from jax.experimental.pallas import tpu as pltpu
from jax.sharding import Mesh, PartitionSpec as P

AXES = ("xh", "zh", "zl", "y", "xl", "c")
SIZES = (2, 8, 2, 4, 2, 2)
LINE = ("zh", "zl")
PLANE = ("xh", "y", "xl")
RING = ("xh", "xl")
FSDP = ("xl", "c")

epsilon = 1e-06
LOG2E = 1.4426950408889634
TOTAL_ROWS = 24576
VMEM_BYTES = 18 * 2**20
BY_COLUMNS = (((1,), (1,)), ((), ()))
BY_ROWS = (((0,), (0,)), ((), ()))

IN_VMEM = pl.BlockSpec(memory_space=pltpu.VMEM)
IN_SMEM = pl.BlockSpec(memory_space=pltpu.SMEM)
ANYWHERE = pl.BlockSpec(memory_space=pl.ANY)
IN_HBM = pl.BlockSpec(memory_space=pltpu.HBM)


def shift(step, size):
    return [(i, (i + step) % size) for i in range(size)]


def along_z(array, step):
    return lax.ppermute(array, LINE, shift(step % 16, 16))


def other_core(array):
    return lax.ppermute(array, "c", shift(1, 2))


def lay(pieces, whole_ref, sems, starts):
    copies = [
        pltpu.make_async_copy(piece, whole_ref.at[pl.ds(start, piece.shape[0])], sems.at[k])
        for k, (piece, start) in enumerate(zip(pieces, starts))
    ]
    for copy in copies:
        copy.start()
    for copy in copies:
        copy.wait()


def unit_kernel(rows_ref, out_ref):
    values = rows_ref[...].astype(jnp.float32)
    norm = jnp.sqrt(jnp.sum(values * values, axis=-1, keepdims=True) + epsilon)
    out_ref[...] = (values / norm).astype(out_ref.dtype)


def unit_rows(rows):
    return pl.pallas_call(
        unit_kernel,
        out_shape=jax.ShapeDtypeStruct(rows.shape, rows.dtype),
        in_specs=[IN_VMEM],
        out_specs=IN_VMEM,
        compiler_params=pltpu.CompilerParams(vmem_limit_bytes=2**21),
    )(rows)


def project_kernel(block, place_ref, from_ref, *refs):
    settings, pieces, refs = refs[:3], refs[3:-7], refs[-7:]
    text_ref, head_ref, pair_ref, scalars_ref, rows_ref, sems, rows_sem = refs
    copy = pltpu.make_async_copy(from_ref, rows_ref, rows_sem)
    copy.start()
    depth = pieces[0].shape[0]
    starts = [pl.multiple_of(place_ref[k] * depth, 32) for k in range(len(pieces))]
    lay(pieces, head_ref, sems, starts)
    copy.wait()
    for start in range(0, rows_ref.shape[0], block):
        at = pl.ds(start, block)
        projected = jnp.dot(rows_ref[at], head_ref[...], preferred_element_type=jnp.float32)
        norm = jnp.sqrt(jnp.sum(projected * projected, axis=-1, keepdims=True) + epsilon)
        text_ref[at] = (projected * (1.0 / norm)).astype(text_ref.dtype)
    coldness, offset, weighting = (setting[...] for setting in settings)
    sharpness = jnp.exp(coldness)
    factor = sharpness * weighting * (1.0 / TOTAL_ROWS)
    raised, log_factor = offset * LOG2E, jnp.log2(factor)
    scalars = [sharpness * LOG2E, -raised - log_factor, raised - log_factor, 1.0 / factor]
    for k, scalar in enumerate(scalars):
        scalars_ref[k : k + 1] = jnp.broadcast_to(scalar, (1, scalars_ref.shape[1]))
    count = pair_ref.shape[0]
    pair_ref[...] = rows_ref[pl.ds(pl.multiple_of(place_ref[len(pieces)] * count, 32), count)]


def project(place, rows, settings, pieces, pair):
    count, width = rows.shape
    return pl.pallas_call(
        functools.partial(project_kernel, count // 2),
        out_shape=[
            jax.ShapeDtypeStruct((count, width), jnp.bfloat16),
            jax.ShapeDtypeStruct((width, width), jnp.bfloat16),
            jax.ShapeDtypeStruct((pair, width), jnp.bfloat16),
            jax.ShapeDtypeStruct((8, 128), jnp.float32),
        ],
        in_specs=[IN_SMEM, IN_HBM] + [IN_VMEM] * 3 + [ANYWHERE] * len(pieces),
        out_specs=[IN_VMEM] * 4,
        scratch_shapes=[
            pltpu.VMEM((count, width), jnp.bfloat16),
            pltpu.SemaphoreType.DMA((len(pieces),)),
            pltpu.SemaphoreType.DMA,
        ],
        compiler_params=pltpu.CompilerParams(vmem_limit_bytes=46 * 2**20),
    )(place, rows, *settings, *pieces)


def meet_kernel(block, own_rows, last, place_ref, text_ref, *refs):
    scalars_ref, refs = refs[0], refs[1:]
    if last:
        pieces, (sum_ref, _, into_ref, images_ref, sems, out_ref, out_sems) = refs[:-7], refs[-7:]
    else:
        pieces, (out_ref, images_ref, sems) = refs[:-3], refs[-3:]
        if not own_rows:
            pieces, sum_ref = pieces[:-1], pieces[-1]
    lay(pieces, images_ref, sems, [sum(p.shape[0] for p in pieces[:k]) for k in range(len(pieces))])
    scale, plus, minus, rest = (scalars_ref[k : k + 1, :1] for k in range(4))

    def result(k):
        at = pl.ds(pl.multiple_of(k * block, block), block)
        return pltpu.make_async_copy(out_ref.at[at], into_ref.at[at], out_sems.at[k])

    def step(k, _):
        at = pl.ds(pl.multiple_of(k * block, block), block)
        cosine = lax.dot_general(
            text_ref[at], images_ref[...], BY_COLUMNS, preferred_element_type=jnp.float32
        )
        weights = 1.0 / (jnp.exp2(plus - cosine * scale) + rest)
        grad = jnp.dot(
            weights.astype(jnp.bfloat16), images_ref[...], preferred_element_type=jnp.float32
        )
        if not own_rows:
            grad = sum_ref[at] + grad
        out_ref[at] = grad.astype(out_ref.dtype)
        if last:
            result(k).start()
        return 0

    steps = text_ref.shape[0] // block
    lax.fori_loop(0, steps, step, 0)
    if own_rows:
        own = pl.ds(pl.multiple_of(place_ref[5], 16), own_rows)
        image = images_ref[pl.ds(pl.multiple_of(place_ref[6], 16), own_rows)].astype(jnp.float32)
        cosine = jnp.sum(text_ref[own].astype(jnp.float32) * image, axis=-1, keepdims=True)
        apart = 1.0 / (jnp.exp2(plus - cosine * scale) + rest)
        paired = -1.0 / (jnp.exp2(cosine * scale + minus) + rest)
        change = paired.astype(jnp.bfloat16).astype(jnp.float32)
        change = change - apart.astype(jnp.bfloat16).astype(jnp.float32)
        out_ref[own] = out_ref[own] + change * image
    if last:
        for k in range(steps):
            result(k).wait()


def meet(scalars, place, text, pieces, total=None, into=None, own_rows=0):
    count, width = text.shape
    images = sum(p.shape[0] for p in pieces)
    last = into is not None
    given = [a for a in (total, into) if a is not None]
    return pl.pallas_call(
        functools.partial(meet_kernel, count // 2, own_rows, last),
        out_shape=jax.ShapeDtypeStruct((count, width), jnp.bfloat16 if last else jnp.float32),
        in_specs=[IN_SMEM, IN_VMEM]
        + [IN_VMEM]
        + [ANYWHERE] * len(pieces)
        + [IN_VMEM, IN_HBM][: len(given)],
        out_specs=IN_HBM if last else IN_VMEM,
        scratch_shapes=[
            pltpu.VMEM((images, width), jnp.bfloat16),
            pltpu.SemaphoreType.DMA((len(pieces),)),
        ]
        + ([pltpu.VMEM((count, width), jnp.bfloat16), pltpu.SemaphoreType.DMA((2,))] if last else []),
        input_output_aliases={4 + len(pieces): 0} if last else {},
        compiler_params=pltpu.CompilerParams(vmem_limit_bytes=VMEM_BYTES),
        cost_estimate=pl.CostEstimate(
            flops=4 * count * images * width,
            bytes_accessed=2 * width * (3 * count + images),
            transcendentals=2 * count * images,
        ),
    )(place, text, scalars, *pieces, *given)


def join_kernel(*refs):
    pieces, (out_ref, sems) = refs[:-3], refs[-2:]
    lay(pieces, out_ref, sems, [sum(p.shape[0] for p in pieces[:k]) for k in range(len(pieces))])


def join(pieces, after):
    count, width = sum(p.shape[0] for p in pieces), pieces[0].shape[1]
    return pl.pallas_call(
        join_kernel,
        out_shape=jax.ShapeDtypeStruct((count, width), jnp.bfloat16),
        in_specs=[ANYWHERE] * (len(pieces) + 1),
        out_specs=ANYWHERE,
        scratch_shapes=[pltpu.SemaphoreType.DMA((len(pieces),))],
        compiler_params=pltpu.CompilerParams(vmem_limit_bytes=2**20),
        cost_estimate=pl.CostEstimate(
            flops=0, bytes_accessed=4 * count * width, transcendentals=0
        ),
    )(*pieces, after)


def finish_kernel(from_ref, projected_ref, out_ref, parts_ref, sems):
    copies = [
        pltpu.make_async_copy(from_ref.at[k], parts_ref.at[k], sems.at[k])
        for k in range(parts_ref.shape[0])
    ]
    for copy in copies:
        copy.start()
    projected = projected_ref[...]
    norm = jnp.sqrt(jnp.sum(projected * projected, axis=-1, keepdims=True) + epsilon)
    unit = projected / norm
    grad = jnp.zeros(unit.shape, jnp.float32)
    for k, copy in enumerate(copies):
        copy.wait()
        grad = grad + parts_ref[k].astype(jnp.float32)
    radial = jnp.sum(unit * grad, axis=-1, keepdims=True)
    out_ref[...] = ((grad - unit * radial) / norm).astype(out_ref.dtype)


def finish(parts, projected):
    return pl.pallas_call(
        finish_kernel,
        out_shape=jax.ShapeDtypeStruct(projected.shape, jnp.bfloat16),
        in_specs=[ANYWHERE, IN_VMEM],
        out_specs=IN_VMEM,
        scratch_shapes=[
            pltpu.VMEM(parts.shape, parts.dtype),
            pltpu.SemaphoreType.DMA((parts.shape[0],)),
        ],
        compiler_params=pltpu.CompilerParams(vmem_limit_bytes=VMEM_BYTES // 2),
    )(parts, projected)


def last_kernel(columns_ref, group_ref, own_ref, from_ref, feat_ref, to_ref, head_ref, grad_ref, sem, to_sem):
    head = pltpu.make_async_copy(from_ref, head_ref, sem)
    head.start()
    grad_ref[...] = lax.dot_general(
        columns_ref[...], group_ref[...], BY_ROWS, preferred_element_type=jnp.float32
    )
    result = pltpu.make_async_copy(grad_ref, to_ref, to_sem)
    result.start()
    head.wait()
    feat_ref[...] = lax.dot_general(
        own_ref[...], head_ref[...], BY_COLUMNS, preferred_element_type=jnp.float32
    ).astype(feat_ref.dtype)
    result.wait()


def last(columns, group_grad, own_grad, head):
    width = head.shape[0]
    return pl.pallas_call(
        last_kernel,
        out_shape=[
            jax.ShapeDtypeStruct(own_grad.shape, jnp.bfloat16),
            jax.ShapeDtypeStruct((columns.shape[1], width), jnp.float32),
        ],
        in_specs=[IN_VMEM] * 3 + [ANYWHERE],
        out_specs=[IN_VMEM, ANYWHERE],
        scratch_shapes=[
            pltpu.VMEM(head.shape, jnp.bfloat16),
            pltpu.VMEM((columns.shape[1], width), jnp.float32),
            pltpu.SemaphoreType.DMA,
            pltpu.SemaphoreType.DMA,
        ],
        compiler_params=pltpu.CompilerParams(vmem_limit_bytes=VMEM_BYTES),
    )(columns, group_grad, own_grad, head)


def body(features, pictures, head_rows, coldness, offset, weighting):
    rows, width = features.shape
    xh, zh, zl, y, xl, c = (lax.axis_index(a) for a in AXES)
    plane = 16
    place = (((xh * 4 + y) * 2 + xl) * rows).astype(jnp.int32)

    plane_features = lax.all_to_all(jnp.tile(features, (plane, 1)), PLANE, 0, 0, tiled=True)

    crossed = lax.ppermute(head_rows, "xl", shift(1, 2))
    at = [xl * 2 + c, (1 - xl) * 2 + c, xl * 2 + 1 - c, (1 - xl) * 2 + 1 - c]
    at += [xh * 4 + y, place, zh * rows]
    places = jnp.stack([a.astype(jnp.int32) for a in at])

    own = unit_rows(pictures)
    even = lax.all_gather(own, "zh", axis=0, tiled=True)
    half = even.shape[0] // 2
    late = [along_z(even[:half], 1), along_z(even[half:], -1)]
    head_pieces = [head_rows, crossed, other_core(head_rows), other_core(crossed)]
    settings = [setting.reshape(1, 1) for setting in (coldness, offset, weighting)]
    text, head, pair, scalars = project(places, plane_features, settings, head_pieces, 2 * rows)

    total = meet(scalars, places, text, [even], own_rows=rows)
    other_line = other_core(join([even] + late, total))
    total = meet(scalars, places, text, late, total)
    partial = meet(scalars, places, text, [other_line], total, plane_features)

    parts = lax.all_to_all(partial, PLANE, 0, 0, tiled=True).reshape(plane, rows, width)

    projected = jnp.dot(features, head, preferred_element_type=jnp.float32)
    other = other_core(pair)
    low, high = jnp.where(c == 0, pair, other), jnp.where(c == 0, other, pair)
    group = jnp.stack([low.reshape(2, rows, width), high.reshape(2, rows, width)], axis=1)
    columns = lax.dynamic_slice_in_dim(
        group.reshape(4 * rows, width), (xl * 2 + c) * (width // 4), width // 4, axis=1
    )

    proj_grad = finish(parts, projected)
    group_grad = lax.all_gather(proj_grad, FSDP, axis=0, tiled=True)
    feat_grad, head_grad = last(columns, group_grad, proj_grad, head)
    return feat_grad, head_grad[None]


def solution(mesh):
    fine = Mesh(mesh.devices.reshape(SIZES), AXES)
    return jax.shard_map(
        body,
        mesh=fine,
        in_specs=(P(AXES, None), P(AXES, None), P(FSDP, None), P(), P(), P()),
        out_specs=(P(AXES, None), P(("xh", "zh", "zl", "y"), FSDP, None)),
        check_vma=False,
    )
```

```python
import functools

import jax
import jax.numpy as jnp
from jax import lax
from jax.experimental import pallas as pl
from jax.experimental.pallas import tpu as pltpu
from jax.sharding import Mesh, PartitionSpec as P

AXES = ("xh", "zh", "zl", "y", "xl", "c")
SIZES = (2, 8, 2, 4, 2, 2)
LINE = ("zh", "zl")
PLANE = ("xh", "y", "xl")
RING = ("xh", "xl")
FSDP = ("xl", "c")

epsilon = 1e-06
LOG2E = 1.4426950408889634
TOTAL_ROWS = 24576
VMEM_BYTES = 18 * 2**20
BY_COLUMNS = (((1,), (1,)), ((), ()))
BY_ROWS = (((0,), (0,)), ((), ()))

IN_VMEM = pl.BlockSpec(memory_space=pltpu.VMEM)
IN_SMEM = pl.BlockSpec(memory_space=pltpu.SMEM)
ANYWHERE = pl.BlockSpec(memory_space=pl.ANY)
IN_HBM = pl.BlockSpec(memory_space=pltpu.HBM)


def shift(step, size):
    return [(i, (i + step) % size) for i in range(size)]


def along_z(array, step):
    return lax.ppermute(array, LINE, shift(step % 16, 16))


def other_core(array):
    return lax.ppermute(array, "c", shift(1, 2))


def lay(pieces, whole_ref, sems, starts):
    copies = [
        pltpu.make_async_copy(piece, whole_ref.at[pl.ds(start, piece.shape[0])], sems.at[k])
        for k, (piece, start) in enumerate(zip(pieces, starts))
    ]
    for copy in copies:
        copy.start()
    for copy in copies:
        copy.wait()


def unit_kernel(rows_ref, out_ref):
    values = rows_ref[...].astype(jnp.float32)
    norm = jnp.sqrt(jnp.sum(values * values, axis=-1, keepdims=True) + epsilon)
    out_ref[...] = (values / norm).astype(out_ref.dtype)


def unit_rows(rows):
    return pl.pallas_call(
        unit_kernel,
        out_shape=jax.ShapeDtypeStruct(rows.shape, rows.dtype),
        in_specs=[IN_VMEM],
        out_specs=IN_VMEM,
        compiler_params=pltpu.CompilerParams(vmem_limit_bytes=2**21),
    )(rows)


def project_kernel(block, place_ref, from_ref, *refs):
    settings, pieces, refs = refs[:3], refs[3:-7], refs[-7:]
    text_ref, head_ref, pair_ref, scalars_ref, rows_ref, sems, rows_sem = refs
    copy = pltpu.make_async_copy(from_ref, rows_ref, rows_sem)
    copy.start()
    depth = pieces[0].shape[0]
    starts = [pl.multiple_of(place_ref[k] * depth, 32) for k in range(len(pieces))]
    lay(pieces, head_ref, sems, starts)
    copy.wait()
    for start in range(0, rows_ref.shape[0], block):
        at = pl.ds(start, block)
        projected = jnp.dot(rows_ref[at], head_ref[...], preferred_element_type=jnp.float32)
        norm = jnp.sqrt(jnp.sum(projected * projected, axis=-1, keepdims=True) + epsilon)
        text_ref[at] = (projected * (1.0 / norm)).astype(text_ref.dtype)
    coldness, offset, weighting = (setting[...] for setting in settings)
    sharpness = jnp.exp(coldness)
    factor = sharpness * weighting * (1.0 / TOTAL_ROWS)
    raised, log_factor = offset * LOG2E, jnp.log2(factor)
    scalars = [sharpness * LOG2E, -raised - log_factor, raised - log_factor, 1.0 / factor]
    for k, scalar in enumerate(scalars):
        scalars_ref[k : k + 1] = jnp.broadcast_to(scalar, (1, scalars_ref.shape[1]))
    count = pair_ref.shape[0]
    pair_ref[...] = rows_ref[pl.ds(pl.multiple_of(place_ref[len(pieces)] * count, 32), count)]


def project(place, rows, settings, pieces, pair):
    count, width = rows.shape
    return pl.pallas_call(
        functools.partial(project_kernel, count // 2),
        out_shape=[
            jax.ShapeDtypeStruct((count, width), jnp.bfloat16),
            jax.ShapeDtypeStruct((width, width), jnp.bfloat16),
            jax.ShapeDtypeStruct((pair, width), jnp.bfloat16),
            jax.ShapeDtypeStruct((8, 128), jnp.float32),
        ],
        in_specs=[IN_SMEM, IN_HBM] + [IN_VMEM] * 3 + [ANYWHERE] * len(pieces),
        out_specs=[IN_VMEM] * 4,
        scratch_shapes=[
            pltpu.VMEM((count, width), jnp.bfloat16),
            pltpu.SemaphoreType.DMA((len(pieces),)),
            pltpu.SemaphoreType.DMA,
        ],
        compiler_params=pltpu.CompilerParams(vmem_limit_bytes=46 * 2**20),
    )(place, rows, *settings, *pieces)


def meet_kernel(block, own_rows, last, place_ref, text_ref, *refs):
    scalars_ref, refs = refs[0], refs[1:]
    if last:
        pieces, (sum_ref, _, into_ref, images_ref, sems, out_ref, out_sems) = refs[:-7], refs[-7:]
    else:
        pieces, (out_ref, images_ref, sems) = refs[:-3], refs[-3:]
        if not own_rows:
            pieces, sum_ref = pieces[:-1], pieces[-1]
    lay(pieces, images_ref, sems, [sum(p.shape[0] for p in pieces[:k]) for k in range(len(pieces))])
    scale, plus, minus, rest = (scalars_ref[k : k + 1, :1] for k in range(4))

    def result(k):
        at = pl.ds(pl.multiple_of(k * block, block), block)
        return pltpu.make_async_copy(out_ref.at[at], into_ref.at[at], out_sems.at[k])

    def step(k, _):
        at = pl.ds(pl.multiple_of(k * block, block), block)
        cosine = lax.dot_general(
            text_ref[at], images_ref[...], BY_COLUMNS, preferred_element_type=jnp.float32
        )
        weights = 1.0 / (jnp.exp2(plus - cosine * scale) + rest)
        grad = jnp.dot(
            weights.astype(jnp.bfloat16), images_ref[...], preferred_element_type=jnp.float32
        )
        if not own_rows:
            grad = sum_ref[at] + grad
        out_ref[at] = grad.astype(out_ref.dtype)
        if last:
            result(k).start()
        return 0

    steps = text_ref.shape[0] // block
    lax.fori_loop(0, steps, step, 0)
    if own_rows:
        own = pl.ds(pl.multiple_of(place_ref[5], 16), own_rows)
        image = images_ref[pl.ds(pl.multiple_of(place_ref[6], 16), own_rows)].astype(jnp.float32)
        cosine = jnp.sum(text_ref[own].astype(jnp.float32) * image, axis=-1, keepdims=True)
        apart = 1.0 / (jnp.exp2(plus - cosine * scale) + rest)
        paired = -1.0 / (jnp.exp2(cosine * scale + minus) + rest)
        change = paired.astype(jnp.bfloat16).astype(jnp.float32)
        change = change - apart.astype(jnp.bfloat16).astype(jnp.float32)
        out_ref[own] = out_ref[own] + change * image
    if last:
        for k in range(steps):
            result(k).wait()


def meet(scalars, place, text, pieces, total=None, into=None, own_rows=0):
    count, width = text.shape
    images = sum(p.shape[0] for p in pieces)
    last = into is not None
    given = [a for a in (total, into) if a is not None]
    return pl.pallas_call(
        functools.partial(meet_kernel, count // 2 if last else count, own_rows, last),
        out_shape=jax.ShapeDtypeStruct((count, width), jnp.bfloat16 if last else jnp.float32),
        in_specs=[IN_SMEM, IN_VMEM]
        + [IN_VMEM]
        + [ANYWHERE] * len(pieces)
        + [IN_VMEM, IN_HBM][: len(given)],
        out_specs=IN_HBM if last else IN_VMEM,
        scratch_shapes=[
            pltpu.VMEM((images, width), jnp.bfloat16),
            pltpu.SemaphoreType.DMA((len(pieces),)),
        ]
        + ([pltpu.VMEM((count, width), jnp.bfloat16), pltpu.SemaphoreType.DMA((2,))] if last else []),
        input_output_aliases={4 + len(pieces): 0} if last else {},
        compiler_params=pltpu.CompilerParams(vmem_limit_bytes=VMEM_BYTES),
        cost_estimate=pl.CostEstimate(
            flops=4 * count * images * width,
            bytes_accessed=2 * width * (3 * count + images),
            transcendentals=2 * count * images,
        ),
    )(place, text, scalars, *pieces, *given)


def join_kernel(*refs):
    pieces, (out_ref, sems) = refs[:-3], refs[-2:]
    lay(pieces, out_ref, sems, [sum(p.shape[0] for p in pieces[:k]) for k in range(len(pieces))])


def join(pieces, after):
    count, width = sum(p.shape[0] for p in pieces), pieces[0].shape[1]
    return pl.pallas_call(
        join_kernel,
        out_shape=jax.ShapeDtypeStruct((count, width), jnp.bfloat16),
        in_specs=[ANYWHERE] * (len(pieces) + 1),
        out_specs=ANYWHERE,
        scratch_shapes=[pltpu.SemaphoreType.DMA((len(pieces),))],
        compiler_params=pltpu.CompilerParams(vmem_limit_bytes=2**20),
        cost_estimate=pl.CostEstimate(
            flops=0, bytes_accessed=4 * count * width, transcendentals=0
        ),
    )(*pieces, after)


def finish_kernel(from_ref, projected_ref, out_ref, parts_ref, sems):
    copies = [
        pltpu.make_async_copy(from_ref.at[k], parts_ref.at[k], sems.at[k])
        for k in range(parts_ref.shape[0])
    ]
    for copy in copies:
        copy.start()
    projected = projected_ref[...]
    norm = jnp.sqrt(jnp.sum(projected * projected, axis=-1, keepdims=True) + epsilon)
    unit = projected / norm
    grad = jnp.zeros(unit.shape, jnp.float32)
    for k, copy in enumerate(copies):
        copy.wait()
        grad = grad + parts_ref[k].astype(jnp.float32)
    radial = jnp.sum(unit * grad, axis=-1, keepdims=True)
    out_ref[...] = ((grad - unit * radial) / norm).astype(out_ref.dtype)


def finish(parts, projected):
    return pl.pallas_call(
        finish_kernel,
        out_shape=jax.ShapeDtypeStruct(projected.shape, jnp.bfloat16),
        in_specs=[ANYWHERE, IN_VMEM],
        out_specs=IN_VMEM,
        scratch_shapes=[
            pltpu.VMEM(parts.shape, parts.dtype),
            pltpu.SemaphoreType.DMA((parts.shape[0],)),
        ],
        compiler_params=pltpu.CompilerParams(vmem_limit_bytes=VMEM_BYTES // 2),
    )(parts, projected)


def last_kernel(columns_ref, group_ref, own_ref, from_ref, feat_ref, to_ref, head_ref, grad_ref, sem, to_sem):
    head = pltpu.make_async_copy(from_ref, head_ref, sem)
    head.start()
    grad_ref[...] = lax.dot_general(
        columns_ref[...], group_ref[...], BY_ROWS, preferred_element_type=jnp.float32
    )
    result = pltpu.make_async_copy(grad_ref, to_ref, to_sem)
    result.start()
    head.wait()
    feat_ref[...] = lax.dot_general(
        own_ref[...], head_ref[...], BY_COLUMNS, preferred_element_type=jnp.float32
    ).astype(feat_ref.dtype)
    result.wait()


def last(columns, group_grad, own_grad, head):
    width = head.shape[0]
    return pl.pallas_call(
        last_kernel,
        out_shape=[
            jax.ShapeDtypeStruct(own_grad.shape, jnp.bfloat16),
            jax.ShapeDtypeStruct((columns.shape[1], width), jnp.float32),
        ],
        in_specs=[IN_VMEM] * 3 + [ANYWHERE],
        out_specs=[IN_VMEM, ANYWHERE],
        scratch_shapes=[
            pltpu.VMEM(head.shape, jnp.bfloat16),
            pltpu.VMEM((columns.shape[1], width), jnp.float32),
            pltpu.SemaphoreType.DMA,
            pltpu.SemaphoreType.DMA,
        ],
        compiler_params=pltpu.CompilerParams(vmem_limit_bytes=VMEM_BYTES),
    )(columns, group_grad, own_grad, head)


def body(features, pictures, head_rows, coldness, offset, weighting):
    rows, width = features.shape
    xh, zh, zl, y, xl, c = (lax.axis_index(a) for a in AXES)
    plane = 16
    place = (((xh * 4 + y) * 2 + xl) * rows).astype(jnp.int32)

    plane_features = lax.all_to_all(jnp.tile(features, (plane, 1)), PLANE, 0, 0, tiled=True)

    crossed = lax.ppermute(head_rows, "xl", shift(1, 2))
    at = [xl * 2 + c, (1 - xl) * 2 + c, xl * 2 + 1 - c, (1 - xl) * 2 + 1 - c]
    at += [xh * 4 + y, place, zh * rows]
    places = jnp.stack([a.astype(jnp.int32) for a in at])

    own = unit_rows(pictures)
    even = lax.all_gather(own, "zh", axis=0, tiled=True)
    half = even.shape[0] // 2
    late = [along_z(even[:half], 1), along_z(even[half:], -1)]
    head_pieces = [head_rows, crossed, other_core(head_rows), other_core(crossed)]
    settings = [setting.reshape(1, 1) for setting in (coldness, offset, weighting)]
    text, head, pair, scalars = project(places, plane_features, settings, head_pieces, 2 * rows)

    total = meet(scalars, places, text, [even], own_rows=rows)
    other_line = other_core(join([even] + late, total))
    total = meet(scalars, places, text, late, total)
    partial = meet(scalars, places, text, [other_line], total, plane_features)

    parts = lax.all_to_all(partial, PLANE, 0, 0, tiled=True).reshape(plane, rows, width)

    projected = jnp.dot(features, head, preferred_element_type=jnp.float32)
    other = other_core(pair)
    low, high = jnp.where(c == 0, pair, other), jnp.where(c == 0, other, pair)
    group = jnp.stack([low.reshape(2, rows, width), high.reshape(2, rows, width)], axis=1)
    columns = lax.dynamic_slice_in_dim(
        group.reshape(4 * rows, width), (xl * 2 + c) * (width // 4), width // 4, axis=1
    )

    proj_grad = finish(parts, projected)
    group_grad = lax.all_gather(proj_grad, FSDP, axis=0, tiled=True)
    feat_grad, head_grad = last(columns, group_grad, proj_grad, head)
    return feat_grad, head_grad[None]


def solution(mesh):
    fine = Mesh(mesh.devices.reshape(SIZES), AXES)
    return jax.shard_map(
        body,
        mesh=fine,
        in_specs=(P(AXES, None), P(AXES, None), P(FSDP, None), P(), P(), P()),
        out_specs=(P(AXES, None), P(("xh", "zh", "zl", "y"), FSDP, None)),
        check_vma=False,
    )
```

```python
import functools

import jax
import jax.numpy as jnp
from jax import lax
from jax.experimental import pallas as pl
from jax.experimental.pallas import tpu as pltpu
from jax.sharding import Mesh, PartitionSpec as P

AXES = ("xh", "zh", "zl", "y", "xl", "c")
SIZES = (2, 8, 2, 4, 2, 2)
LINE = ("zh", "zl")
PLANE = ("xh", "y", "xl")
RING = ("xh", "xl")
FSDP = ("xl", "c")

epsilon = 1e-06
LOG2E = 1.4426950408889634
TOTAL_ROWS = 24576
VMEM_BYTES = 18 * 2**20
BY_COLUMNS = (((1,), (1,)), ((), ()))
BY_ROWS = (((0,), (0,)), ((), ()))

IN_VMEM = pl.BlockSpec(memory_space=pltpu.VMEM)
IN_SMEM = pl.BlockSpec(memory_space=pltpu.SMEM)
ANYWHERE = pl.BlockSpec(memory_space=pl.ANY)
IN_HBM = pl.BlockSpec(memory_space=pltpu.HBM)


def shift(step, size):
    return [(i, (i + step) % size) for i in range(size)]


def along_z(array, step):
    return lax.ppermute(array, LINE, shift(step % 16, 16))


def other_core(array):
    return lax.ppermute(array, "c", shift(1, 2))


def lay(pieces, whole_ref, sems, starts):
    copies = [
        pltpu.make_async_copy(piece, whole_ref.at[pl.ds(start, piece.shape[0])], sems.at[k])
        for k, (piece, start) in enumerate(zip(pieces, starts))
    ]
    for copy in copies:
        copy.start()
    for copy in copies:
        copy.wait()


def unit_kernel(rows_ref, out_ref):
    values = rows_ref[...].astype(jnp.float32)
    norm = jnp.sqrt(jnp.sum(values * values, axis=-1, keepdims=True) + epsilon)
    out_ref[...] = (values / norm).astype(out_ref.dtype)


def unit_rows(rows):
    return pl.pallas_call(
        unit_kernel,
        out_shape=jax.ShapeDtypeStruct(rows.shape, rows.dtype),
        in_specs=[IN_VMEM],
        out_specs=IN_VMEM,
        compiler_params=pltpu.CompilerParams(vmem_limit_bytes=2**21),
    )(rows)


def project_kernel(block, place_ref, from_ref, *refs):
    settings, pieces, refs = refs[:3], refs[3:-7], refs[-7:]
    text_ref, head_ref, pair_ref, scalars_ref, rows_ref, sems, rows_sem = refs
    copy = pltpu.make_async_copy(from_ref, rows_ref, rows_sem)
    copy.start()
    depth = pieces[0].shape[0]
    starts = [pl.multiple_of(place_ref[k] * depth, 32) for k in range(len(pieces))]
    lay(pieces, head_ref, sems, starts)
    copy.wait()
    for start in range(0, rows_ref.shape[0], block):
        at = pl.ds(start, block)
        projected = jnp.dot(rows_ref[at], head_ref[...], preferred_element_type=jnp.float32)
        norm = jnp.sqrt(jnp.sum(projected * projected, axis=-1, keepdims=True) + epsilon)
        text_ref[at] = (projected * (1.0 / norm)).astype(text_ref.dtype)
    coldness, offset, weighting = (setting[...] for setting in settings)
    sharpness = jnp.exp(coldness)
    factor = sharpness * weighting * (1.0 / TOTAL_ROWS)
    raised, log_factor = offset * LOG2E, jnp.log2(factor)
    scalars = [sharpness * LOG2E, -raised - log_factor, raised - log_factor, 1.0 / factor]
    for k, scalar in enumerate(scalars):
        scalars_ref[k : k + 1] = jnp.broadcast_to(scalar, (1, scalars_ref.shape[1]))
    count = pair_ref.shape[0]
    pair_ref[...] = rows_ref[pl.ds(pl.multiple_of(place_ref[len(pieces)] * count, 32), count)]


def project(place, rows, settings, pieces, pair):
    count, width = rows.shape
    return pl.pallas_call(
        functools.partial(project_kernel, count // 2),
        out_shape=[
            jax.ShapeDtypeStruct((count, width), jnp.bfloat16),
            jax.ShapeDtypeStruct((width, width), jnp.bfloat16),
            jax.ShapeDtypeStruct((pair, width), jnp.bfloat16),
            jax.ShapeDtypeStruct((8, 128), jnp.float32),
        ],
        in_specs=[IN_SMEM, IN_HBM] + [IN_VMEM] * 3 + [ANYWHERE] * len(pieces),
        out_specs=[IN_VMEM] * 4,
        scratch_shapes=[
            pltpu.VMEM((count, width), jnp.bfloat16),
            pltpu.SemaphoreType.DMA((len(pieces),)),
            pltpu.SemaphoreType.DMA,
        ],
        compiler_params=pltpu.CompilerParams(vmem_limit_bytes=46 * 2**20),
    )(place, rows, *settings, *pieces)


def meet_kernel(block, own_rows, last, place_ref, text_ref, *refs):
    scalars_ref, refs = refs[0], refs[1:]
    if last:
        pieces, (sum_ref, _, into_ref, images_ref, sems, out_ref, out_sems) = refs[:-7], refs[-7:]
    else:
        pieces, (out_ref, images_ref, sems) = refs[:-3], refs[-3:]
        if not own_rows:
            pieces, sum_ref = pieces[:-1], pieces[-1]
    lay(pieces, images_ref, sems, [sum(p.shape[0] for p in pieces[:k]) for k in range(len(pieces))])
    scale, plus, minus, rest = (scalars_ref[k : k + 1, :1] for k in range(4))

    def result(k):
        at = pl.ds(pl.multiple_of(k * block, block), block)
        return pltpu.make_async_copy(out_ref.at[at], into_ref.at[at], out_sems.at[k])

    def step(k, _):
        at = pl.ds(pl.multiple_of(k * block, block), block)
        cosine = lax.dot_general(
            text_ref[at], images_ref[...], BY_COLUMNS, preferred_element_type=jnp.float32
        )
        weights = 1.0 / (jnp.exp2(plus - cosine * scale) + rest)
        grad = jnp.dot(
            weights.astype(jnp.bfloat16), images_ref[...], preferred_element_type=jnp.float32
        )
        if not own_rows:
            grad = sum_ref[at] + grad
        out_ref[at] = grad.astype(out_ref.dtype)
        if last:
            result(k).start()
        return 0

    steps = text_ref.shape[0] // block
    lax.fori_loop(0, steps, step, 0, unroll=True)
    if own_rows:
        own = pl.ds(pl.multiple_of(place_ref[5], 16), own_rows)
        image = images_ref[pl.ds(pl.multiple_of(place_ref[6], 16), own_rows)].astype(jnp.float32)
        cosine = jnp.sum(text_ref[own].astype(jnp.float32) * image, axis=-1, keepdims=True)
        apart = 1.0 / (jnp.exp2(plus - cosine * scale) + rest)
        paired = -1.0 / (jnp.exp2(cosine * scale + minus) + rest)
        change = paired.astype(jnp.bfloat16).astype(jnp.float32)
        change = change - apart.astype(jnp.bfloat16).astype(jnp.float32)
        out_ref[own] = out_ref[own] + change * image
    if last:
        for k in range(steps):
            result(k).wait()


def meet(scalars, place, text, pieces, total=None, into=None, own_rows=0):
    count, width = text.shape
    images = sum(p.shape[0] for p in pieces)
    last = into is not None
    given = [a for a in (total, into) if a is not None]
    return pl.pallas_call(
        functools.partial(meet_kernel, count // 2 if last else count, own_rows, last),
        out_shape=jax.ShapeDtypeStruct((count, width), jnp.bfloat16 if last else jnp.float32),
        in_specs=[IN_SMEM, IN_VMEM]
        + [IN_VMEM]
        + [ANYWHERE] * len(pieces)
        + [IN_VMEM, IN_HBM][: len(given)],
        out_specs=IN_HBM if last else IN_VMEM,
        scratch_shapes=[
            pltpu.VMEM((images, width), jnp.bfloat16),
            pltpu.SemaphoreType.DMA((len(pieces),)),
        ]
        + ([pltpu.VMEM((count, width), jnp.bfloat16), pltpu.SemaphoreType.DMA((2,))] if last else []),
        input_output_aliases={4 + len(pieces): 0} if last else {},
        compiler_params=pltpu.CompilerParams(vmem_limit_bytes=VMEM_BYTES),
        cost_estimate=pl.CostEstimate(
            flops=4 * count * images * width,
            bytes_accessed=2 * width * (3 * count + images),
            transcendentals=2 * count * images,
        ),
    )(place, text, scalars, *pieces, *given)


def join_kernel(*refs):
    pieces, (out_ref, sems) = refs[:-3], refs[-2:]
    lay(pieces, out_ref, sems, [sum(p.shape[0] for p in pieces[:k]) for k in range(len(pieces))])


def join(pieces, after):
    count, width = sum(p.shape[0] for p in pieces), pieces[0].shape[1]
    return pl.pallas_call(
        join_kernel,
        out_shape=jax.ShapeDtypeStruct((count, width), jnp.bfloat16),
        in_specs=[ANYWHERE] * (len(pieces) + 1),
        out_specs=ANYWHERE,
        scratch_shapes=[pltpu.SemaphoreType.DMA((len(pieces),))],
        compiler_params=pltpu.CompilerParams(vmem_limit_bytes=2**20),
        cost_estimate=pl.CostEstimate(
            flops=0, bytes_accessed=4 * count * width, transcendentals=0
        ),
    )(*pieces, after)


def finish_kernel(from_ref, projected_ref, out_ref, parts_ref, sems):
    copies = [
        pltpu.make_async_copy(from_ref.at[k], parts_ref.at[k], sems.at[k])
        for k in range(parts_ref.shape[0])
    ]
    for copy in copies:
        copy.start()
    projected = projected_ref[...]
    norm = jnp.sqrt(jnp.sum(projected * projected, axis=-1, keepdims=True) + epsilon)
    unit = projected / norm
    grad = jnp.zeros(unit.shape, jnp.float32)
    for k, copy in enumerate(copies):
        copy.wait()
        grad = grad + parts_ref[k].astype(jnp.float32)
    radial = jnp.sum(unit * grad, axis=-1, keepdims=True)
    out_ref[...] = ((grad - unit * radial) / norm).astype(out_ref.dtype)


def finish(parts, projected):
    return pl.pallas_call(
        finish_kernel,
        out_shape=jax.ShapeDtypeStruct(projected.shape, jnp.bfloat16),
        in_specs=[ANYWHERE, IN_VMEM],
        out_specs=IN_VMEM,
        scratch_shapes=[
            pltpu.VMEM(parts.shape, parts.dtype),
            pltpu.SemaphoreType.DMA((parts.shape[0],)),
        ],
        compiler_params=pltpu.CompilerParams(vmem_limit_bytes=VMEM_BYTES // 2),
    )(parts, projected)


def last_kernel(columns_ref, group_ref, own_ref, from_ref, feat_ref, to_ref, head_ref, grad_ref, sem, to_sem):
    head = pltpu.make_async_copy(from_ref, head_ref, sem)
    head.start()
    grad_ref[...] = lax.dot_general(
        columns_ref[...], group_ref[...], BY_ROWS, preferred_element_type=jnp.float32
    )
    result = pltpu.make_async_copy(grad_ref, to_ref, to_sem)
    result.start()
    head.wait()
    feat_ref[...] = lax.dot_general(
        own_ref[...], head_ref[...], BY_COLUMNS, preferred_element_type=jnp.float32
    ).astype(feat_ref.dtype)
    result.wait()


def last(columns, group_grad, own_grad, head):
    width = head.shape[0]
    return pl.pallas_call(
        last_kernel,
        out_shape=[
            jax.ShapeDtypeStruct(own_grad.shape, jnp.bfloat16),
            jax.ShapeDtypeStruct((columns.shape[1], width), jnp.float32),
        ],
        in_specs=[IN_VMEM] * 3 + [ANYWHERE],
        out_specs=[IN_VMEM, ANYWHERE],
        scratch_shapes=[
            pltpu.VMEM(head.shape, jnp.bfloat16),
            pltpu.VMEM((columns.shape[1], width), jnp.float32),
            pltpu.SemaphoreType.DMA,
            pltpu.SemaphoreType.DMA,
        ],
        compiler_params=pltpu.CompilerParams(vmem_limit_bytes=VMEM_BYTES),
    )(columns, group_grad, own_grad, head)


def body(features, pictures, head_rows, coldness, offset, weighting):
    rows, width = features.shape
    xh, zh, zl, y, xl, c = (lax.axis_index(a) for a in AXES)
    plane = 16
    place = (((xh * 4 + y) * 2 + xl) * rows).astype(jnp.int32)

    plane_features = lax.all_to_all(jnp.tile(features, (plane, 1)), PLANE, 0, 0, tiled=True)

    crossed = lax.ppermute(head_rows, "xl", shift(1, 2))
    at = [xl * 2 + c, (1 - xl) * 2 + c, xl * 2 + 1 - c, (1 - xl) * 2 + 1 - c]
    at += [xh * 4 + y, place, zh * rows]
    places = jnp.stack([a.astype(jnp.int32) for a in at])

    own = unit_rows(pictures)
    even = lax.all_gather(own, "zh", axis=0, tiled=True)
    half = even.shape[0] // 2
    late = [along_z(even[:half], 1), along_z(even[half:], -1)]
    head_pieces = [head_rows, crossed, other_core(head_rows), other_core(crossed)]
    settings = [setting.reshape(1, 1) for setting in (coldness, offset, weighting)]
    text, head, pair, scalars = project(places, plane_features, settings, head_pieces, 2 * rows)

    total = meet(scalars, places, text, [even], own_rows=rows)
    other_line = other_core(join([even] + late, total))
    total = meet(scalars, places, text, late, total)
    partial = meet(scalars, places, text, [other_line], total, plane_features)

    parts = lax.all_to_all(partial, PLANE, 0, 0, tiled=True).reshape(plane, rows, width)

    projected = jnp.dot(features, head, preferred_element_type=jnp.float32)
    other = other_core(pair)
    low, high = jnp.where(c == 0, pair, other), jnp.where(c == 0, other, pair)
    group = jnp.stack([low.reshape(2, rows, width), high.reshape(2, rows, width)], axis=1)
    columns = lax.dynamic_slice_in_dim(
        group.reshape(4 * rows, width), (xl * 2 + c) * (width // 4), width // 4, axis=1
    )

    proj_grad = finish(parts, projected)
    group_grad = lax.all_gather(proj_grad, FSDP, axis=0, tiled=True)
    feat_grad, head_grad = last(columns, group_grad, proj_grad, head)
    return feat_grad, head_grad[None]


def solution(mesh):
    fine = Mesh(mesh.devices.reshape(SIZES), AXES)
    return jax.shard_map(
        body,
        mesh=fine,
        in_specs=(P(AXES, None), P(AXES, None), P(FSDP, None), P(), P(), P()),
        out_specs=(P(AXES, None), P(("xh", "zh", "zl", "y"), FSDP, None)),
        check_vma=False,
    )
```
